128 devices in a mesh: row: 8 (over z, y_lo), col: 16 (over x, y_hi, core).
Axes of the slice: x: 4, y: 4 (y_hi: 2, y_lo: 2; y = y_hi * 2 + y_lo), z: 4, core: 2. Of those that a mesh axis runs over, the one named last changes fastest.
Arguments:
- tile_values: bfloat16 [8, 16, 128, 128, 128], P('row', 'col'), may hold values from -0.125 to 0.125
- tile_rows: int32 [8, 16, 128], P('row', 'col'), may hold values from 0 to 63
- tile_cols: int32 [8, 16, 128], P('row', 'col'), may hold values from 0 to 31
- tile_counts: int32 [8, 16], P('row', 'col'), may hold values from 16 to 128, as said below
- features: bfloat16 [65536, 256], P(('col', 'row')), may hold values from -6 to 6
- weight: bfloat16 [256, 256], replicated, may hold values from -0.375 to 0.375
- cotangent: bfloat16 [65536, 256], P(('row', 'col')), may hold values from -6 to 6
Outputs:
- output: bfloat16 [65536, 256], P(('row', 'col'))
- grad_features: bfloat16 [65536, 256], P(('col', 'row'))
- weight_grad: float32 [256, 256], replicated
The draws below stay inside these ranges and needn't reach their ends.
Inputs may be any that keep to these rules, and one draw needn't show every extreme that they name: `tile_counts`: every grid cell lists at least 16 tiles, and at least one cell in every draw lists 128; slots past a cell's count hold entries that are no part of the adjacency.
All inputs are finite; a program needn't handle non-finite values.
Results may differ from the reference program's by a relative error of at most 0.024.
Values may be sent and summed in bfloat16 or wider, within the bound.
No kernel may reach another device: no remote copies, remote signals or barrier semaphores. Data moves between devices by JAX's collectives and lax.ppermute only.
A program may use at most 128 MiB of HBM per device.

```python
import jax
import jax.numpy as jnp
from jax import lax

WIDTH = 256
BLK = 128
TILE_CAP = 128
NODES = 65536
ROW_BLOCKS = 64
COL_BLOCKS = 32
N_ROW = 8
N_COL = 16


def draw_tile_counts(key, part):
    key = jax.random.fold_in(key, 11)
    key_base, key_order = jax.random.split(key)
    cells = N_ROW * N_COL
    base_count = jax.random.randint(key_base, (cells,), TILE_CAP // 8, TILE_CAP // 2 + 1)
    shuffled = jax.random.permutation(key_order, cells)
    full_cell = shuffled < max(1, cells // 8)
    counts = jnp.where(full_cell, TILE_CAP, base_count)
    return counts.reshape(N_ROW, N_COL).astype(jnp.int32)


def set_ends(drawn, key, smallest, top_value):
    dims = drawn.shape
    index_at = [jax.random.randint(jax.random.fold_in(key, axis), (), 0, dims[axis]) for axis in range(len(dims))]
    drawn = drawn.at[tuple(index_at)].set(smallest)
    longest = dims.index(max(dims))
    index_at[longest] = (index_at[longest] + 1) % dims[longest]
    return drawn.at[tuple(index_at)].set(top_value)


def shard_levels(rng, extent, cuts, low, high):
    gain, own = 1.0, jax.random.fold_in(rng, 6)
    for dim, blocks in cuts:
        steps = jnp.exp(jax.random.uniform(jax.random.fold_in(own, dim), (blocks,), jnp.float32, low / len(cuts), high / len(cuts)))
        gain = gain * jnp.repeat(steps, extent[dim] // blocks).reshape([-1 if axis == dim else 1 for axis in range(len(extent))])
    return gain


def scatter_about(key, shape, spread, bound, cuts=(), kind=jnp.bfloat16):
    factor_of = shard_levels(key, shape, cuts, -0.22, 0.18) if cuts else 1.0
    values = jax.random.normal(key, shape, jnp.float32) * spread * factor_of
    return jnp.minimum(jnp.maximum(values, -bound), bound).astype(kind)


def setup_inputs(seed: int = 0) -> dict:
    key_of = jax.random.split(jax.random.key(seed), 8)
    tile_values = scatter_about(key_of[0], (N_ROW, N_COL, TILE_CAP, BLK, BLK), (BLK * 16) ** -0.5, 0.125, ((0, 8), (1, 16)))
    tile_rows = set_ends(jax.random.randint(key_of[1], (N_ROW, N_COL, TILE_CAP), 0, ROW_BLOCKS), jax.random.fold_in(key_of[1], 1), 0, ROW_BLOCKS - 1).astype(jnp.int32)
    tile_cols = set_ends(jax.random.randint(key_of[2], (N_ROW, N_COL, TILE_CAP), 0, COL_BLOCKS), jax.random.fold_in(key_of[2], 1), 0, COL_BLOCKS - 1).astype(jnp.int32)
    tile_counts = draw_tile_counts(jax.random.fold_in(key_of[7], 71), 0)
    features = scatter_about(key_of[4], (NODES, WIDTH), 1.0, 6.0, ((0, 128),))
    weight = scatter_about(key_of[5], (WIDTH, WIDTH), WIDTH ** -0.5, 0.375)
    cotangent = scatter_about(key_of[6], (NODES, WIDTH), 1.0, 6.0, ((0, 128),))
    return {"tile_values": tile_values, "tile_rows": tile_rows, "tile_cols": tile_cols, "tile_counts": tile_counts, "features": features, "weight": weight, "cotangent": cotangent}


def cell_forward(blocks, tile_row, tile_col, tile_total, feature_blocks):
    live_slots = (jnp.arange(blocks.shape[0]) < tile_total).astype(jnp.float32)
    picked = feature_blocks[tile_col].astype(jnp.float32)
    products = jnp.einsum('kab,kbw->kaw', blocks.astype(jnp.float32), picked) * live_slots[:, None, None]
    return jax.ops.segment_sum(products, tile_row, num_segments=ROW_BLOCKS)

def cell_backward(blocks, tile_row, tile_col, tile_total, grad_blocks):
    live_slots = (jnp.arange(blocks.shape[0]) < tile_total).astype(jnp.float32)
    picked = grad_blocks[tile_row].astype(jnp.float32)
    products = jnp.einsum('kab,kaw->kbw', blocks.astype(jnp.float32), picked) * live_slots[:, None, None]
    return jax.ops.segment_sum(products, tile_col, num_segments=COL_BLOCKS)

def reference(tile_values, tile_rows, tile_cols, tile_counts, features, weight, cotangent):
    feat_width = features.shape[1]
    feat_groups = features.reshape(N_COL, COL_BLOCKS, BLK, feat_width)

    def row_group(row_index):

        def add_cell(running, col_index):
            part = cell_forward(tile_values[row_index, col_index], tile_rows[row_index, col_index], tile_cols[row_index, col_index], tile_counts[row_index, col_index], feat_groups[col_index])
            rounded = lax.optimization_barrier(part.astype(jnp.bfloat16))
            return (running + rounded.astype(jnp.float32), None)
        start = jnp.zeros((ROW_BLOCKS, BLK, feat_width), jnp.float32)
        running, unused = lax.scan(add_cell, start, jnp.arange(N_COL, dtype=jnp.int32))
        return running.astype(jnp.bfloat16)
    agg = lax.map(row_group, jnp.arange(N_ROW, dtype=jnp.int32)).reshape(NODES, feat_width)
    pre_act = jnp.dot(agg, weight, preferred_element_type=jnp.float32)
    sigmoid_pre = jax.nn.sigmoid(pre_act)
    output = (pre_act * sigmoid_pre).astype(jnp.bfloat16)
    grad_pre = (cotangent.astype(jnp.float32) * sigmoid_pre * (1.0 + pre_act * (1.0 - sigmoid_pre))).astype(jnp.bfloat16)
    weight_grad = jnp.dot(agg.T, grad_pre, preferred_element_type=jnp.float32) / jnp.sqrt(jnp.float32(NODES))
    grad_agg = jnp.dot(grad_pre, weight.T, preferred_element_type=jnp.float32).astype(jnp.bfloat16)
    grad_groups = grad_agg.reshape(N_ROW, ROW_BLOCKS, BLK, feat_width)

    def col_group(col_index):

        def add_cell(running, row_index):
            part = cell_backward(tile_values[row_index, col_index], tile_rows[row_index, col_index], tile_cols[row_index, col_index], tile_counts[row_index, col_index], grad_groups[row_index])
            rounded = lax.optimization_barrier(part.astype(jnp.bfloat16))
            return (running + rounded.astype(jnp.float32), None)
        start = jnp.zeros((COL_BLOCKS, BLK, feat_width), jnp.float32)
        running, unused = lax.scan(add_cell, start, jnp.arange(N_ROW, dtype=jnp.int32))
        return running.astype(jnp.bfloat16)
    grad_features = lax.map(col_group, jnp.arange(N_COL, dtype=jnp.int32)).reshape(NODES, feat_width)
    return (output, grad_features, weight_grad)
```

```python
import functools
import math

import jax
import jax.numpy as jnp
from jax import lax
from jax.experimental import pallas as pl
from jax.experimental.pallas import tpu as pltpu
from jax.sharding import PartitionSpec as P

BLK = 128
WIDTH = 256
CAP = 128
UNROLL = 4
CHUNKS = 4
BF16 = jnp.bfloat16
F32 = jnp.float32

NZ, NX = 4, 4


def z_perm(step):
    return [(z * 2 + yl, (z + step) % NZ * 2 + yl) for z in range(NZ) for yl in range(2)]


def yl_perm():
    return [(r, r ^ 1) for r in range(2 * NZ)]


def x_perm(step):
    return [(x * 4 + q, (x + step) % NX * 4 + q) for x in range(NX) for q in range(4)]


def yh_perm():
    return [(c, c ^ 2) for c in range(4 * NX)]


def core_perm():
    return [(c, c ^ 1) for c in range(4 * NX)]


def z_send(v, step):
    return lax.ppermute(v, "row", z_perm(step))


def yl_swap(v):
    return lax.ppermute(v, "row", yl_perm())


def x_send(v, step):
    return lax.ppermute(v, "col", x_perm(step))


def yh_swap(v):
    return lax.ppermute(v, "col", yh_perm())


def core_swap(v):
    return lax.ppermute(v, "col", core_perm())


def add(*terms):
    total = terms[0].astype(F32)
    for term in terms[1:]:
        total = total + term.astype(F32)
    return total.astype(BF16)


def tile_loop(count, tiles_hbm, tiles, tile_sems, step, acc, product):
    size = CAP // CHUNKS
    for chunk in range(CHUNKS):
        pltpu.make_async_copy(
            tiles_hbm.at[pl.ds(chunk * size, size)],
            tiles.at[pl.ds(chunk * size, size)],
            tile_sems.at[chunk],
        ).wait()
        live = jnp.clip(count - chunk * size, 0, size)
        groups = live // UNROLL

        def group(i, carry):
            first = chunk * size + i * UNROLL
            parts = [product(first + u) for u in range(UNROLL)]
            for u in range(UNROLL):
                slot = step[first + u]
                acc[slot] += parts[u]
            return carry

        lax.fori_loop(0, groups, group, 0)

        def single(i, carry):
            k = chunk * size + i
            acc[step[k]] += product(k)
            return carry

        lax.fori_loop(groups * UNROLL, live, single, 0)


def start_tiles(tiles_hbm, tiles, tile_sems):
    size = CAP // CHUNKS
    for chunk in range(CHUNKS):
        pltpu.make_async_copy(
            tiles_hbm.at[pl.ds(chunk * size, size)],
            tiles.at[pl.ds(chunk * size, size)],
            tile_sems.at[chunk],
        ).start()


def clear(acc):
    def body(i, carry):
        acc[i] = jnp.zeros(acc.shape[1:], acc.dtype)
        return carry

    lax.fori_loop(0, acc.shape[0], body, 0)


def cell_kernel(transposed, places, n_out, out_ref, in_ref, cnt_ref, tiles_hbm, *rest):
    n_in = len(places)
    pieces = rest[:n_in]
    outs = rest[n_in : n_in + n_out]
    tiles, blocks, acc, tile_sems, piece_sems = rest[n_in + n_out :]
    copies = []
    for i, (piece, (first, size)) in enumerate(zip(pieces, places)):
        copy = pltpu.make_async_copy(piece, blocks.at[pl.ds(first, size)], piece_sems.at[i])
        copy.start()
        copies.append(copy)
    start_tiles(tiles_hbm, tiles, tile_sems)
    clear(acc)
    for copy in copies:
        copy.wait()
    count = cnt_ref[0]
    dims = (((0,), (0,)), ((), ())) if transposed else (((1,), (0,)), ((), ()))

    def product(k):
        return lax.dot_general(
            tiles[k], blocks[in_ref[k]], dims, preferred_element_type=F32
        )

    tile_loop(count, tiles_hbm, tiles, tile_sems, out_ref, acc, product)
    first = 0
    for out in outs:
        def store(i, carry, out=out, first=first):
            out[i] = acc[first + i].astype(BF16)
            return carry

        lax.fori_loop(0, out.shape[0], store, 0)
        first += out.shape[0]


def cell_product(name, transposed, out_slot, in_slot, count, tiles, pieces, places, out_sizes, in_blocks):
    out_blocks = sum(out_sizes)
    kernel = functools.partial(cell_kernel, transposed, places, len(out_sizes))
    any_spec = pl.BlockSpec(memory_space=pl.ANY)
    vmem_spec = pl.BlockSpec(memory_space=pltpu.VMEM)
    return pl.pallas_call(
        kernel,
        grid_spec=pltpu.PrefetchScalarGridSpec(
            num_scalar_prefetch=3,
            grid=(),
            in_specs=[any_spec] * (1 + len(pieces)),
            out_specs=[vmem_spec] * len(out_sizes),
            scratch_shapes=[
                pltpu.VMEM((CAP, BLK, BLK), BF16),
                pltpu.VMEM((in_blocks, BLK, WIDTH), BF16),
                pltpu.VMEM((out_blocks, BLK, WIDTH), F32),
                pltpu.SemaphoreType.DMA((CHUNKS,)),
                pltpu.SemaphoreType.DMA((len(pieces),)),
            ],
        ),
        out_shape=[jax.ShapeDtypeStruct((n, BLK, WIDTH), BF16) for n in out_sizes],
        compiler_params=pltpu.CompilerParams(vmem_limit_bytes=48 * 1024 * 1024),
        cost_estimate=pl.CostEstimate(
            flops=2 * CAP * BLK * BLK * WIDTH,
            bytes_accessed=2 * CAP * BLK * BLK + 2 * (in_blocks + out_blocks) * BLK * WIDTH,
            transcendentals=0,
        ),
        name=name,
    )(out_slot, in_slot, count, tiles, *pieces)


def dense_kernel(scale, a0, a1, b0, b1, b2, b3, w_ref, cot_ref, out_ref, ga_ref, gb_ref, wg_ref):
    rows = 2 * BLK
    w = w_ref[...]
    terms = ((a0, a1), (b0, b1, b2, b3))
    weight_grad = None
    for half in range(2):
        total = terms[half][0][...].astype(F32)
        for term in terms[half][1:]:
            total = total + term[...].astype(F32)
        agg = total.astype(BF16).reshape(rows, WIDTH)
        pre = jnp.dot(agg, w, preferred_element_type=F32)
        sig = jax.nn.sigmoid(pre)
        span = pl.ds(half * rows, rows)
        out_ref[span, :] = (pre * sig).astype(BF16)
        grad_pre = (cot_ref[span, :].astype(F32) * sig * (1.0 + pre * (1.0 - sig))).astype(BF16)
        grad_agg = lax.dot_general(
            grad_pre, w, (((1,), (1,)), ((), ())), preferred_element_type=F32
        ).astype(BF16)
        (ga_ref, gb_ref)[half][...] = grad_agg.reshape(2, BLK, WIDTH)
        term = lax.dot_general(
            agg, grad_pre, (((0,), (0,)), ((), ())), preferred_element_type=F32
        )
        weight_grad = term if weight_grad is None else weight_grad + term
    wg_ref[...] = weight_grad * scale


def dense(scale, parts, weight, cotangent):
    vmem_spec = pl.BlockSpec(memory_space=pltpu.VMEM)
    nodes = cotangent.shape[0]
    return pl.pallas_call(
        functools.partial(dense_kernel, scale),
        in_specs=[vmem_spec] * 8,
        out_specs=[vmem_spec] * 4,
        out_shape=[
            jax.ShapeDtypeStruct((nodes, WIDTH), BF16),
            jax.ShapeDtypeStruct((2, BLK, WIDTH), BF16),
            jax.ShapeDtypeStruct((2, BLK, WIDTH), BF16),
            jax.ShapeDtypeStruct((WIDTH, WIDTH), F32),
        ],
        compiler_params=pltpu.CompilerParams(vmem_limit_bytes=32 * 1024 * 1024),
        cost_estimate=pl.CostEstimate(
            flops=6 * nodes * WIDTH * WIDTH,
            bytes_accessed=8 * nodes * WIDTH,
            transcendentals=nodes * WIDTH,
        ),
        name="dense",
    )(*parts, weight, cotangent)


def gather_row(features):
    own = features.reshape(4, BLK, WIDTH)
    a, b = own[:2], own[2:]
    a_y = yl_swap(a)
    b_z = [z_send(b, -d) for d in (1, 3, 2)]
    a_z = [z_send(a, -d) for d in (1, 3, 2)]
    a_yz = [z_send(a_y, -d) for d in (1, 3, 2)]
    b_y = [yl_swap(v) for v in [b] + b_z]
    pieces, places = [a, a_y, b, b_y[0]], [(0, 2), (2, 2), (16, 2), (18, 2)]
    for i, d in enumerate((1, 3, 2)):
        pieces += [a_z[i], a_yz[i], b_z[i], b_y[i + 1]]
        places += [(d * 4, 2), (d * 4 + 2, 2), (16 + d * 4, 2), (16 + d * 4 + 2, 2)]
    return pieces, places


def gather_col(ga, gb):
    b_y = yh_swap(gb)
    a_x = [x_send(ga, -d) for d in (1, 3, 2)]
    b_x = [x_send(gb, -d) for d in (1, 3, 2)]
    b_yx = [x_send(b_y, -d) for d in (1, 3, 2)]
    a_y = [yh_swap(v) for v in [ga] + a_x]
    a_all = jnp.concatenate(
        [ga, a_y[0], a_x[0], a_y[1], a_x[2], a_y[3], a_x[1], a_y[2]], axis=0
    )
    b_all = jnp.concatenate(
        [gb, b_y, b_x[0], b_yx[0], b_x[2], b_yx[2], b_x[1], b_yx[1]], axis=0
    )
    pieces = [a_all, b_all, core_swap(a_all), core_swap(b_all)]
    return pieces, [(0, 16), (16, 16), (32, 16), (48, 16)]


def scatter_col(mine, other):
    recv = core_swap(other)
    total = add(mine, recv)
    a = [total[4 * d : 4 * d + 4] for d in range(4)]
    b0, b1 = total[16:24], total[24:32]
    r = [x_send(a[d], d) for d in (1, 3, 2)]
    q = yh_swap(b1)
    s = add(a[0], *r)
    u = add(b0, q)
    c = yh_swap(s[2:4])
    e = [x_send(u[2 * d : 2 * d + 2], d) for d in (1, 3, 2)]
    return s[:2], c, u[:2], *e


def scatter_row(a0, a1, a2, a3, b0, b1):
    r = [z_send(v, d) for v, d in ((a1, 1), (a3, 3), (a2, 2))]
    q = yl_swap(b1)
    s = add(a0, *r)
    u = add(b0, q)
    c = yl_swap(s[2:4])
    e = [z_send(u[2 * d : 2 * d + 2], d) for d in (1, 3, 2)]
    first = add(s[:2], c)
    second = add(u[:2], *e)
    return jnp.concatenate([first, second], axis=0).reshape(4 * BLK, WIDTH)


def ring_sum(own, send):
    opposite, left, right = send(own, 2), send(own, 1), send(own, -1)
    return (own + opposite) + (left + right)


def y_send(v, step):
    pairs = []
    for r in range(2 * NZ):
        for c in range(4 * NX):
            y = ((c // 2 % 2) * 2 + r % 2 + step) % 4
            to = (r - r % 2 + y % 2) * (4 * NX) + c - (c & 2) + (y // 2) * 2
            pairs.append((r * 4 * NX + c, to))
    return lax.ppermute(v, ("row", "col"), pairs)


def sum_everywhere(term, core):
    half = WIDTH // 2
    mine = lax.dynamic_slice_in_dim(term, core * half, half, 0)
    other = lax.dynamic_slice_in_dim(term, (1 - core) * half, half, 0)
    total = mine + core_swap(other)
    total = ring_sum(total, x_send)
    total = ring_sum(total, z_send)
    total = ring_sum(total, y_send)
    far = core_swap(total)
    first = jnp.where(core == 0, total, far)
    second = jnp.where(core == 0, far, total)
    return jnp.concatenate([first, second], axis=0)


def shards(tile_values, tile_rows, tile_cols, tile_counts, features, weight, cotangent):
    row, col = lax.axis_index("row"), lax.axis_index("col")
    z, yl = row // 2, row % 2
    x, yh, core = col // 4, col // 2 % 2, col % 2
    tiles = tile_values[0, 0]
    t_row, t_col = tile_rows[0, 0], tile_cols[0, 0]
    count = tile_counts[0]

    own, j = t_row // 4, t_row % 4
    dx, dyh, dk = (own // 4 - x) % 4, (own // 2 % 2) ^ yh, (own % 2) ^ core
    h, jj = j // 2, j % 2
    row_out = dk * 32 + h * 16 + jj + jnp.where(h == 0, dx * 4 + dyh * 2, dyh * 8 + dx * 2)
    row_in = dk * 32 + h * 16 + dx * 4 + dyh * 2 + jj

    own, j = t_col // 4, t_col % 4
    dz, dyl = (own // 2 - z) % 4, (own % 2) ^ yl
    h, jj = j // 2, j % 2
    col_out = h * 16 + jj + jnp.where(h == 0, dz * 4 + dyl * 2, dyl * 8 + dz * 2)
    col_in = h * 16 + dz * 4 + dyl * 2 + jj

    pieces, places = gather_row(features)
    mine, other = cell_product(
        "forward_cell", False, row_out, col_in, count, tiles, pieces, places, [32, 32], 32
    )
    parts = scatter_col(mine, other)
    scale = 1.0 / math.sqrt(features.shape[0] * lax.axis_size("row") * lax.axis_size("col"))
    output, ga, gb, local_grad = dense(scale, parts, weight, cotangent)
    weight_grad = sum_everywhere(local_grad, core)
    pieces, places = gather_col(ga, gb)
    back = cell_product(
        "backward_cell", True, col_out, row_in, count, tiles, pieces, places, [4, 4, 4, 4, 8, 8], 64
    )
    grad_features = scatter_row(*back)
    return (output, grad_features, weight_grad)


def solution(mesh):
    in_specs = (
        P("row", "col", None, None, None),
        P("row", "col", None),
        P("row", "col", None),
        P("row", "col"),
        P(("col", "row"), None),
        P(),
        P(("row", "col"), None),
    )
    out_specs = (P(("row", "col"), None), P(("col", "row"), None), P())
    return jax.shard_map(shards, mesh=mesh, in_specs=in_specs, out_specs=out_specs, check_vma=False)
```

```python
import functools
import math

import jax
import jax.numpy as jnp
from jax import lax
from jax.experimental import pallas as pl
from jax.experimental.pallas import tpu as pltpu
from jax.sharding import PartitionSpec as P

BLK = 128
WIDTH = 256
CAP = 128
UNROLL = 16
BF16 = jnp.bfloat16
F32 = jnp.float32

NZ, NX = 4, 4


def z_perm(step):
    return [(z * 2 + yl, (z + step) % NZ * 2 + yl) for z in range(NZ) for yl in range(2)]


def yl_perm():
    return [(r, r ^ 1) for r in range(2 * NZ)]


def x_perm(step):
    return [(x * 4 + q, (x + step) % NX * 4 + q) for x in range(NX) for q in range(4)]


def yh_perm():
    return [(c, c ^ 2) for c in range(4 * NX)]


def core_perm():
    return [(c, c ^ 1) for c in range(4 * NX)]


def z_send(v, step):
    return lax.ppermute(v, "row", z_perm(step))


def yl_swap(v):
    return lax.ppermute(v, "row", yl_perm())


def x_send(v, step):
    return lax.ppermute(v, "col", x_perm(step))


def yh_swap(v):
    return lax.ppermute(v, "col", yh_perm())


def core_swap(v):
    return lax.ppermute(v, "col", core_perm())


def add(*terms):
    total = terms[0].astype(F32)
    for term in terms[1:]:
        total = total + term.astype(F32)
    return total.astype(BF16)


def cell_kernel(transposed, places, n_out, out_ref, in_ref, cnt_ref, tiles, *rest):
    n_in = len(places)
    pieces = rest[:n_in]
    outs = rest[n_in : n_in + n_out]
    blocks, acc, piece_sems = rest[n_in + n_out :]
    copies = []
    for i, (piece, (first, size)) in enumerate(zip(pieces, places)):
        copy = pltpu.make_async_copy(piece, blocks.at[pl.ds(first, size)], piece_sems.at[i])
        copy.start()
        copies.append(copy)

    def clear(i, carry):
        acc[i] = jnp.zeros(acc.shape[1:], acc.dtype)
        return carry

    lax.fori_loop(0, acc.shape[0] - 1, clear, 0)
    for copy in copies:
        copy.wait()
    dims = (((0,), (0,)), ((), ())) if transposed else (((1,), (0,)), ((), ()))

    def group(i, carry):
        first = i * UNROLL
        products = [
            lax.dot_general(
                tiles[first + u], blocks[in_ref[first + u]], dims, preferred_element_type=F32
            )
            for u in range(UNROLL)
        ]
        for u in range(UNROLL):
            slot = out_ref[first + u]
            acc[slot] += products[u]
        return carry

    lax.fori_loop(0, (cnt_ref[0] + UNROLL - 1) // UNROLL, group, 0)
    first = 0
    for out in outs:
        def store(i, carry, out=out, first=first):
            out[i] = acc[first + i].astype(BF16)
            return carry

        lax.fori_loop(0, out.shape[0], store, 0)
        first += out.shape[0]


def cell_product(name, transposed, out_slot, in_slot, count, tiles, pieces, places, out_sizes, in_blocks):
    out_blocks = sum(out_sizes)
    live = jnp.arange(CAP, dtype=jnp.int32) < count[0]
    out_slot = jnp.where(live, out_slot, out_blocks)
    in_slot = jnp.where(live, in_slot, 0)
    kernel = functools.partial(cell_kernel, transposed, places, len(out_sizes))
    any_spec = pl.BlockSpec(memory_space=pl.ANY)
    vmem_spec = pl.BlockSpec(memory_space=pltpu.VMEM)
    return pl.pallas_call(
        kernel,
        grid_spec=pltpu.PrefetchScalarGridSpec(
            num_scalar_prefetch=3,
            grid=(),
            in_specs=[vmem_spec] + [any_spec] * len(pieces),
            out_specs=[vmem_spec] * len(out_sizes),
            scratch_shapes=[
                pltpu.VMEM((in_blocks, BLK, WIDTH), BF16),
                pltpu.VMEM((out_blocks + 1, BLK, WIDTH), F32),
                pltpu.SemaphoreType.DMA((len(pieces),)),
            ],
        ),
        out_shape=[jax.ShapeDtypeStruct((n, BLK, WIDTH), BF16) for n in out_sizes],
        compiler_params=pltpu.CompilerParams(vmem_limit_bytes=24 * 1024 * 1024),
        cost_estimate=pl.CostEstimate(
            flops=2 * CAP * BLK * BLK * WIDTH,
            bytes_accessed=2 * CAP * BLK * BLK + 2 * (in_blocks + out_blocks) * BLK * WIDTH,
            transcendentals=0,
        ),
        name=name,
    )(out_slot, in_slot, count, tiles, *pieces)


def dense_kernel(scale, n_terms, *refs):
    terms, (w_ref, cot_ref, out_ref, grad_ref, wg_ref) = refs[:n_terms], refs[n_terms:]
    total = terms[0][...].astype(F32)
    for term in terms[1:]:
        total = total + term[...].astype(F32)
    w = w_ref[...]
    agg = total.astype(BF16).reshape(cot_ref.shape)
    pre = jnp.dot(agg, w, preferred_element_type=F32)
    sig = jax.nn.sigmoid(pre)
    out_ref[...] = (pre * sig).astype(BF16)
    grad_pre = (cot_ref[...].astype(F32) * sig * (1.0 + pre * (1.0 - sig))).astype(BF16)
    grad_agg = lax.dot_general(
        grad_pre, w, (((1,), (1,)), ((), ())), preferred_element_type=F32
    ).astype(BF16)
    grad_ref[...] = grad_agg.reshape(grad_ref.shape)
    weight_grad = lax.dot_general(
        agg, grad_pre, (((0,), (0,)), ((), ())), preferred_element_type=F32
    )
    wg_ref[...] = weight_grad * scale


def dense(scale, terms, weight, cotangent):
    vmem_spec = pl.BlockSpec(memory_space=pltpu.VMEM)
    nodes = cotangent.shape[0]
    return pl.pallas_call(
        functools.partial(dense_kernel, scale, len(terms)),
        in_specs=[vmem_spec] * (len(terms) + 2),
        out_specs=[vmem_spec] * 3,
        out_shape=[
            jax.ShapeDtypeStruct((nodes, WIDTH), BF16),
            jax.ShapeDtypeStruct((nodes // BLK, BLK, WIDTH), BF16),
            jax.ShapeDtypeStruct((WIDTH, WIDTH), F32),
        ],
        compiler_params=pltpu.CompilerParams(vmem_limit_bytes=24 * 1024 * 1024),
        cost_estimate=pl.CostEstimate(
            flops=6 * nodes * WIDTH * WIDTH,
            bytes_accessed=8 * nodes * WIDTH,
            transcendentals=nodes * WIDTH,
        ),
        name="dense",
    )(*terms, weight, cotangent)


def gather(own, ring, swap, first_ties=(), second_ties=()):
    far = swap(own)
    up, down, across = ring(own, -1), ring(own, 1), ring(own, 2)
    far_up, far_down = ring(far, -1), ring(far, 1)
    far_across = swap(across)
    return [own, far, up, far_up, across, far_across, down, far_down]


def scatter_terms(chunks, ring, swap):
    two = swap(add(*chunks[2][1]))
    up, down = ring(add(*chunks[1][1]), 1), ring(add(*chunks[3][1]), -1)
    own_up, own_down = ring(add(*chunks[1][0]), 1), ring(add(*chunks[3][0]), -1)
    across = ring(add(*chunks[2][0], two), 2)
    far = swap(add(*chunks[0][1], up, down))
    return [*chunks[0][0], own_up, own_down, across, far]


def y_send(v, step):
    pairs = []
    for r in range(2 * NZ):
        for c in range(4 * NX):
            y = ((c // 2 % 2) * 2 + r % 2 + step) % 4
            to = (r - r % 2 + y % 2) * (4 * NX) + c - (c & 2) + (y // 2) * 2
            pairs.append((r * 4 * NX + c, to))
    return lax.ppermute(v, ("row", "col"), pairs)


def pair_perm(extent, stride, bit):
    return [(i, i ^ (stride * bit)) for i in range(extent)]


def tie(*arrays):
    return lax.optimization_barrier(arrays)


def pair_sum(v, axis, flip):
    return v + lax.ppermute(v, axis, [(i, i ^ flip) for i in range(lax.axis_size(axis))])


def shards(tile_values, tile_rows, tile_cols, tile_counts, features, weight, cotangent):
    row, col = lax.axis_index("row"), lax.axis_index("col")
    z, yl = row // 2, row % 2
    x, yh, core = col // 4, col // 2 % 2, col % 2
    tiles = tile_values[0, 0]
    t_row, t_col = tile_rows[0, 0], tile_cols[0, 0]
    count = tile_counts[0]

    own, j = t_row // 4, t_row % 4
    dx, dyh, dk = (own // 4 - x) % 4, (own // 2 % 2) ^ yh, (own % 2) ^ core
    row_slot = dk * 32 + dx * 8 + dyh * 4 + j
    own, j = t_col // 4, t_col % 4
    dz, dyl = (own // 2 - z) % 4, (own % 2) ^ yl
    col_slot = dz * 8 + dyl * 4 + j
    places = [(4 * i, 4) for i in range(16)]

    pieces = gather(features.reshape(4, BLK, WIDTH), z_send, yl_swap)
    parts = cell_product(
        "forward_cell", False, row_slot, col_slot, count, tiles, pieces, places[:8], [4] * 16, 32
    )
    mine, other = parts[:8], [core_swap(v) for v in parts[8:]]
    chunks = [[(mine[2 * d + s], other[2 * d + s]) for s in range(2)] for d in range(4)]
    terms = scatter_terms(chunks, x_send, yh_swap)
    scale = 1.0 / math.sqrt(features.shape[0] * lax.axis_size("row") * lax.axis_size("col"))
    output, grad_agg, local_grad = dense(scale, terms, weight, cotangent)

    half = WIDTH // 2
    term = lax.dynamic_slice_in_dim(local_grad, core * half, half, 0)
    term = term + core_swap(lax.dynamic_slice_in_dim(local_grad, (1 - core) * half, half, 0))
    term = pair_sum(term, "row", 2)
    pieces = gather(grad_agg, x_send, yh_swap)
    term = pair_sum(term, "row", 4)
    pieces = pieces + [core_swap(v) for v in pieces]
    term = pair_sum(term, "row", 1)
    term, *pieces = tie(term, *pieces)
    back = cell_product(
        "backward_cell", True, col_slot, row_slot, count, tiles, pieces, places, [4] * 8, 64
    )
    term = pair_sum(term, "col", 2)
    term, *back = tie(term, *back)
    term = pair_sum(term, "col", 4)
    term = pair_sum(term, "col", 8)
    far_term = core_swap(term)
    weight_grad = jnp.concatenate(
        [jnp.where(core == 0, term, far_term), jnp.where(core == 0, far_term, term)], axis=0
    )
    chunks = [[(back[2 * d + s],) for s in range(2)] for d in range(4)]
    grad_features = add(*scatter_terms(chunks, z_send, yl_swap))
    return (output, grad_features.reshape(4 * BLK, WIDTH), weight_grad)


def solution(mesh):
    in_specs = (
        P("row", "col", None, None, None),
        P("row", "col", None),
        P("row", "col", None),
        P("row", "col"),
        P(("col", "row"), None),
        P(),
        P(("row", "col"), None),
    )
    out_specs = (P(("row", "col"), None), P(("col", "row"), None), P())
    return jax.shard_map(shards, mesh=mesh, in_specs=in_specs, out_specs=out_specs, check_vma=False)
```

```python
import functools
import math

import jax
import jax.numpy as jnp
from jax import lax
from jax.experimental import pallas as pl
from jax.experimental.pallas import tpu as pltpu
from jax.sharding import PartitionSpec as P

BLK = 128
WIDTH = 256
CAP = 128
UNROLL = 16
CHUNKS = 4
BF16 = jnp.bfloat16
F32 = jnp.float32

NZ, NX = 4, 4


def z_perm(step):
    return [(z * 2 + yl, (z + step) % NZ * 2 + yl) for z in range(NZ) for yl in range(2)]


def yl_perm():
    return [(r, r ^ 1) for r in range(2 * NZ)]


def x_perm(step):
    return [(x * 4 + q, (x + step) % NX * 4 + q) for x in range(NX) for q in range(4)]


def yh_perm():
    return [(c, c ^ 2) for c in range(4 * NX)]


def core_perm():
    return [(c, c ^ 1) for c in range(4 * NX)]


def z_send(v, step):
    return lax.ppermute(v, "row", z_perm(step))


def yl_swap(v):
    return lax.ppermute(v, "row", yl_perm())


def x_send(v, step):
    return lax.ppermute(v, "col", x_perm(step))


def yh_swap(v):
    return lax.ppermute(v, "col", yh_perm())


def core_swap(v):
    return lax.ppermute(v, "col", core_perm())


def add(*terms):
    total = terms[0].astype(F32)
    for term in terms[1:]:
        total = total + term.astype(F32)
    return total.astype(BF16)


def tile_copies(tiles_hbm, tiles, sems):
    size = CAP // CHUNKS
    return [
        pltpu.make_async_copy(
            tiles_hbm.at[pl.ds(c * size, size)], tiles.at[pl.ds(c * size, size)], sems.at[c]
        )
        for c in range(CHUNKS)
    ]


def cell_kernel(transposed, n_in, n_out, out_ref, in_ref, cnt_ref, tiles_hbm, *rest):
    pieces = rest[:n_in]
    outs = rest[n_in : n_in + n_out]
    tiles, blocks, acc, tile_sems, piece_sems = rest[n_in + n_out :]
    copies = [
        pltpu.make_async_copy(piece, blocks.at[pl.ds(4 * i, 4)], piece_sems.at[i])
        for i, piece in enumerate(pieces)
    ]
    loads = tile_copies(tiles_hbm, tiles, tile_sems)
    for copy in copies[:1] + loads[:1] + copies[1:] + loads[1:]:
        copy.start()

    def clear(i, carry):
        acc[i] = jnp.zeros(acc.shape[1:], acc.dtype)
        return carry

    lax.fori_loop(0, acc.shape[0] - 1, clear, 0)
    for copy in copies:
        copy.wait()
    dims = (((0,), (0,)), ((), ())) if transposed else (((1,), (0,)), ((), ()))

    def group(i, carry):
        first = i * UNROLL
        products = [
            lax.dot_general(
                tiles[first + u], blocks[in_ref[first + u]], dims, preferred_element_type=F32
            )
            for u in range(UNROLL)
        ]
        for u in range(UNROLL):
            slot = out_ref[first + u]
            acc[slot] += products[u]
        return carry

    groups = (cnt_ref[0] + UNROLL - 1) // UNROLL
    size = CAP // CHUNKS // UNROLL
    for c, load in enumerate(loads):
        load.wait()
        lax.fori_loop(c * size, jnp.clip(groups, c * size, (c + 1) * size), group, 0)
    for o, out in enumerate(outs):
        def store(i, carry, out=out, o=o):
            out[i] = acc[4 * o + i].astype(BF16)
            return carry

        lax.fori_loop(0, 4, store, 0)


def cell_product(name, transposed, out_slot, in_slot, count, tiles, pieces, n_out):
    live = jnp.arange(CAP, dtype=jnp.int32) < count[0]
    out_slot = jnp.where(live, out_slot, 4 * n_out)
    in_slot = jnp.where(live, in_slot, 0)
    any_spec = pl.BlockSpec(memory_space=pl.ANY)
    vmem_spec = pl.BlockSpec(memory_space=pltpu.VMEM)
    return pl.pallas_call(
        functools.partial(cell_kernel, transposed, len(pieces), n_out),
        grid_spec=pltpu.PrefetchScalarGridSpec(
            num_scalar_prefetch=3,
            grid=(),
            in_specs=[any_spec] * (1 + len(pieces)),
            out_specs=[vmem_spec] * n_out,
            scratch_shapes=[
                pltpu.VMEM((CAP, BLK, BLK), BF16),
                pltpu.VMEM((4 * len(pieces), BLK, WIDTH), BF16),
                pltpu.VMEM((4 * n_out + 1, BLK, WIDTH), F32),
                pltpu.SemaphoreType.DMA((CHUNKS,)),
                pltpu.SemaphoreType.DMA((len(pieces),)),
            ],
        ),
        out_shape=[jax.ShapeDtypeStruct((4, BLK, WIDTH), BF16)] * n_out,
        compiler_params=pltpu.CompilerParams(vmem_limit_bytes=16 * 1024 * 1024),
        cost_estimate=pl.CostEstimate(
            flops=2 * CAP * BLK * BLK * WIDTH,
            bytes_accessed=2 * CAP * BLK * BLK + 8 * (len(pieces) + n_out) * BLK * WIDTH,
            transcendentals=0,
        ),
        name=name,
    )(out_slot, in_slot, count, pltpu.with_memory_space_constraint(tiles, pltpu.HBM), *pieces)


def dense_kernel(scale, n_terms, *refs):
    terms, (w_ref, cot_ref, out_ref, grad_ref, rider_ref) = refs[:n_terms], refs[n_terms:]
    total = terms[0][...].astype(F32)
    for term in terms[1:]:
        total = total + term[...].astype(F32)
    w = w_ref[...]
    agg = total.astype(BF16).reshape(cot_ref.shape)
    pre = jnp.dot(agg, w, preferred_element_type=F32)
    sig = jax.nn.sigmoid(pre)
    out_ref[...] = (pre * sig).astype(BF16)
    grad_pre = (cot_ref[...].astype(F32) * sig * (1.0 + pre * (1.0 - sig))).astype(BF16)
    grad_agg = lax.dot_general(
        grad_pre, w, (((1,), (1,)), ((), ())), preferred_element_type=F32
    ).astype(BF16)
    grad_agg = grad_agg.reshape(grad_ref.shape)
    grad_ref[...] = grad_agg
    rider_ref[pl.ds(0, 4)] = grad_agg
    weight_grad = lax.dot_general(
        agg, grad_pre, (((0,), (0,)), ((), ())), preferred_element_type=F32
    )
    rider_ref[pl.ds(4, 2)] = (weight_grad * scale).astype(BF16).reshape(2, BLK, WIDTH)


def dense(scale, terms, weight, cotangent):
    vmem_spec = pl.BlockSpec(memory_space=pltpu.VMEM)
    nodes = cotangent.shape[0]
    return pl.pallas_call(
        functools.partial(dense_kernel, scale, len(terms)),
        in_specs=[vmem_spec] * (len(terms) + 2),
        out_specs=[vmem_spec] * 3,
        out_shape=[
            jax.ShapeDtypeStruct((nodes, WIDTH), BF16),
            jax.ShapeDtypeStruct((nodes // BLK, BLK, WIDTH), BF16),
            jax.ShapeDtypeStruct((nodes // BLK + 2, BLK, WIDTH), BF16),
        ],
        compiler_params=pltpu.CompilerParams(vmem_limit_bytes=24 * 1024 * 1024),
        cost_estimate=pl.CostEstimate(
            flops=6 * nodes * WIDTH * WIDTH,
            bytes_accessed=8 * nodes * WIDTH,
            transcendentals=nodes * WIDTH,
        ),
        name="dense",
    )(*terms, weight, cotangent)


def after(value, *earlier):
    return lax.optimization_barrier((value, *earlier))[0]


def ring_sum(own, send):
    across, up, down = send(own, 2), send(own, 1), send(own, -1)
    return (own.astype(F32) + across.astype(F32)) + (up.astype(F32) + down.astype(F32))


def shards(tile_values, tile_rows, tile_cols, tile_counts, features, weight, cotangent):
    row, col = lax.axis_index("row"), lax.axis_index("col")
    z, yl = row // 2, row % 2
    x, yh, core = col // 4, col // 2 % 2, col % 2
    tiles = tile_values[0, 0]
    t_row, t_col = tile_rows[0, 0], tile_cols[0, 0]
    count = tile_counts[0]

    own, j = t_row // 4, t_row % 4
    dx, dyh, dk = (own // 4 - x) % 4, (own // 2 % 2) ^ yh, (own % 2) ^ core
    row_slot = dk * 32 + dx * 8 + dyh * 4 + j
    own, j = t_col // 4, t_col % 4
    dz, dyl = (own // 2 - z) % 4, (own % 2) ^ yl
    col_slot = dz * 8 + dyl * 4 + j

    own = features.reshape(4, BLK, WIDTH)
    far = yl_swap(own)
    across = z_send(own, 2)
    up, down = z_send(own, -1), z_send(own, 1)
    far_up, far_down = z_send(far, -1), z_send(far, 1)
    far_across = yl_swap(across)
    own = pltpu.with_memory_space_constraint(own, pltpu.HBM)
    pieces = [own, far, up, far_up, across, far_across, down, far_down]

    parts = cell_product("forward_cell", False, row_slot, col_slot, count, tiles, pieces, 16)
    mine = parts[:8]
    other = [None] * 8
    for i in (5, 3, 7):
        other[i] = core_swap(parts[8 + i])
    for i in (2, 6, 4, 1, 0):
        other[i] = core_swap(after(parts[8 + i], other[7]))
    two = yh_swap(add(mine[5], other[5]))
    up, down = x_send(add(mine[3], other[3]), 1), x_send(add(mine[7], other[7]), -1)
    own_up, own_down = x_send(add(mine[2], other[2]), 1), x_send(add(mine[6], other[6]), -1)
    across = x_send(add(mine[4], other[4], two), 2)
    far = yh_swap(add(mine[1], other[1], up, down))
    terms = [mine[0], other[0], own_up, own_down, across, far]
    scale = 1.0 / math.sqrt(features.shape[0] * lax.axis_size("row") * lax.axis_size("col"))
    output, own, own_rider = dense(scale, terms, weight, cotangent)

    far_rider = yh_swap(own_rider)
    far = far_rider[:4]
    across = x_send(own, 2)
    up, down = x_send(own, -1), x_send(own, 1)
    far_up, far_down = x_send(far, -1), x_send(far, 1)
    far_across = yh_swap(across)
    pieces = [own, far, up, far_up, across, far_across, down, far_down]
    far_rider, *ready = lax.optimization_barrier((far_rider, *pieces))
    term = add(own_rider[4:], far_rider[4:])
    term = add(term, yl_swap(term))
    pieces = [*ready, *(core_swap(v) for v in ready)]
    term = add(term, core_swap(term))
    term = ring_sum(term, z_send).astype(BF16)
    back = cell_product("backward_cell", True, col_slot, row_slot, count, tiles, pieces, 8)
    two = yl_swap(back[5])
    up, down = z_send(back[3], 1), z_send(back[7], -1)
    own_up, own_down = z_send(back[2], 1), z_send(back[6], -1)
    across = z_send(add(back[4], two), 2)
    far = yl_swap(add(back[1], up, down))
    grad_features = add(back[0], own_up, own_down, across, far)
    weight_grad = ring_sum(after(term, up, down), x_send).reshape(WIDTH, WIDTH)
    return (output, grad_features.reshape(4 * BLK, WIDTH), weight_grad)


def solution(mesh):
    in_specs = (
        P("row", "col", None, None, None),
        P("row", "col", None),
        P("row", "col", None),
        P("row", "col"),
        P(("col", "row"), None),
        P(),
        P(("row", "col"), None),
    )
    out_specs = (P(("row", "col"), None), P(("col", "row"), None), P())
    return jax.shard_map(shards, mesh=mesh, in_specs=in_specs, out_specs=out_specs, check_vma=False)
```

```python
import functools
import math

import jax
import jax.numpy as jnp
from jax import lax
from jax.experimental import pallas as pl
from jax.experimental.pallas import tpu as pltpu
from jax.sharding import PartitionSpec as P

BLK = 128
WIDTH = 256
CAP = 128
UNROLL = 32
CHUNKS = 4
BF16 = jnp.bfloat16
F32 = jnp.float32

NZ, NX = 4, 4


def z_perm(step):
    return [(z * 2 + yl, (z + step) % NZ * 2 + yl) for z in range(NZ) for yl in range(2)]


def yl_perm():
    return [(r, r ^ 1) for r in range(2 * NZ)]


def x_perm(step):
    return [(x * 4 + q, (x + step) % NX * 4 + q) for x in range(NX) for q in range(4)]


def yh_perm():
    return [(c, c ^ 2) for c in range(4 * NX)]


def core_perm():
    return [(c, c ^ 1) for c in range(4 * NX)]


def z_send(v, step):
    return lax.ppermute(v, "row", z_perm(step))


def z_pair(v, flip):
    return lax.ppermute(v, "row", [(r, r ^ (2 * flip)) for r in range(2 * NZ)])


def yl_swap(v):
    return lax.ppermute(v, "row", yl_perm())


def x_send(v, step):
    return lax.ppermute(v, "col", x_perm(step))


def yh_swap(v):
    return lax.ppermute(v, "col", yh_perm())


def core_swap(v):
    return lax.ppermute(v, "col", core_perm())


def add(*terms):
    total = terms[0].astype(F32)
    for term in terms[1:]:
        total = total + term.astype(F32)
    return total.astype(BF16)


def tile_copies(tiles_hbm, tiles, sems):
    size = CAP // CHUNKS
    return [
        pltpu.make_async_copy(
            tiles_hbm.at[pl.ds(c * size, size)], tiles.at[pl.ds(c * size, size)], sems.at[c]
        )
        for c in range(CHUNKS)
    ]


def cell_kernel(transposed, n_in, n_out, out_ref, in_ref, cnt_ref, tiles_hbm, *rest):
    pieces = rest[:n_in]
    outs = rest[n_in : n_in + n_out]
    tiles, blocks, acc, tile_sems, piece_sems = rest[n_in + n_out :]
    copies = [
        pltpu.make_async_copy(piece, blocks.at[pl.ds(4 * i, 4)], piece_sems.at[i])
        for i, piece in enumerate(pieces)
    ]
    loads = tile_copies(tiles_hbm, tiles, tile_sems)
    for copy in copies[:1] + loads[:1] + copies[1:] + loads[1:]:
        copy.start()

    def clear(i, carry):
        acc[i] = jnp.zeros(acc.shape[1:], acc.dtype)
        return carry

    lax.fori_loop(0, acc.shape[0] - 1, clear, 0)
    for copy in copies:
        copy.wait()
    dims = (((0,), (0,)), ((), ())) if transposed else (((1,), (0,)), ((), ()))

    def group(i, carry):
        first = i * UNROLL
        for u in range(UNROLL):
            slot = out_ref[first + u]
            acc[slot] += lax.dot_general(
                tiles[first + u], blocks[in_ref[first + u]], dims, preferred_element_type=F32
            )
        return carry

    groups = (cnt_ref[0] + UNROLL - 1) // UNROLL
    size = CAP // CHUNKS // UNROLL
    for c, load in enumerate(loads):
        load.wait()
        lax.fori_loop(c * size, jnp.clip(groups, c * size, (c + 1) * size), group, 0)
    for o, out in enumerate(outs):
        def store(i, carry, out=out, o=o):
            out[i] = acc[4 * o + i].astype(BF16)
            return carry

        lax.fori_loop(0, 4, store, 0)


def cell_product(name, transposed, out_slot, in_slot, count, tiles, pieces, n_out):
    live = jnp.arange(CAP, dtype=jnp.int32) < count[0]
    out_slot = jnp.where(live, out_slot, 4 * n_out)
    in_slot = jnp.where(live, in_slot, 0)
    any_spec = pl.BlockSpec(memory_space=pl.ANY)
    vmem_spec = pl.BlockSpec(memory_space=pltpu.VMEM)
    return pl.pallas_call(
        functools.partial(cell_kernel, transposed, len(pieces), n_out),
        grid_spec=pltpu.PrefetchScalarGridSpec(
            num_scalar_prefetch=3,
            grid=(),
            in_specs=[any_spec] * (1 + len(pieces)),
            out_specs=[vmem_spec] * n_out,
            scratch_shapes=[
                pltpu.VMEM((CAP, BLK, BLK), BF16),
                pltpu.VMEM((4 * len(pieces), BLK, WIDTH), BF16),
                pltpu.VMEM((4 * n_out + 1, BLK, WIDTH), F32),
                pltpu.SemaphoreType.DMA((CHUNKS,)),
                pltpu.SemaphoreType.DMA((len(pieces),)),
            ],
        ),
        out_shape=[jax.ShapeDtypeStruct((4, BLK, WIDTH), BF16)] * n_out,
        compiler_params=pltpu.CompilerParams(vmem_limit_bytes=(19 if len(pieces) == 8 else 16) * 1024 * 1024),
        cost_estimate=pl.CostEstimate(
            flops=2 * CAP * BLK * BLK * WIDTH,
            bytes_accessed=2 * CAP * BLK * BLK + 8 * (len(pieces) + n_out) * BLK * WIDTH,
            transcendentals=0,
        ),
        name=name,
    )(out_slot, in_slot, count, pltpu.with_memory_space_constraint(tiles, pltpu.HBM), *pieces)


def dense_kernel(scale, n_terms, *refs):
    terms, (w_ref, cot_ref, out_ref, grad_ref, rider_ref) = refs[:n_terms], refs[n_terms:]
    total = terms[0][...].astype(F32)
    for term in terms[1:]:
        total = total + term[...].astype(F32)
    w = w_ref[...]
    agg = total.astype(BF16).reshape(cot_ref.shape)
    pre = jnp.dot(agg, w, preferred_element_type=F32)
    sig = jax.nn.sigmoid(pre)
    out_ref[...] = (pre * sig).astype(BF16)
    grad_pre = (cot_ref[...].astype(F32) * sig * (1.0 + pre * (1.0 - sig))).astype(BF16)
    grad_agg = lax.dot_general(
        grad_pre, w, (((1,), (1,)), ((), ())), preferred_element_type=F32
    ).astype(BF16)
    grad_agg = grad_agg.reshape(grad_ref.shape)
    grad_ref[...] = grad_agg
    rider_ref[pl.ds(0, 4)] = grad_agg
    weight_grad = lax.dot_general(
        agg, grad_pre, (((0,), (0,)), ((), ())), preferred_element_type=F32
    )
    rider_ref[pl.ds(4, 2)] = (weight_grad * scale).astype(BF16).reshape(2, BLK, WIDTH)


def dense(scale, terms, weight, cotangent):
    vmem_spec = pl.BlockSpec(memory_space=pltpu.VMEM)
    nodes = cotangent.shape[0]
    return pl.pallas_call(
        functools.partial(dense_kernel, scale, len(terms)),
        in_specs=[vmem_spec] * (len(terms) + 2),
        out_specs=[vmem_spec] * 3,
        out_shape=[
            jax.ShapeDtypeStruct((nodes, WIDTH), BF16),
            jax.ShapeDtypeStruct((nodes // BLK, BLK, WIDTH), BF16),
            jax.ShapeDtypeStruct((nodes // BLK + 2, BLK, WIDTH), BF16),
        ],
        compiler_params=pltpu.CompilerParams(vmem_limit_bytes=24 * 1024 * 1024),
        cost_estimate=pl.CostEstimate(
            flops=6 * nodes * WIDTH * WIDTH,
            bytes_accessed=8 * nodes * WIDTH,
            transcendentals=nodes * WIDTH,
        ),
        name="dense",
    )(*terms, weight, cotangent)


def after(value, *earlier):
    return lax.optimization_barrier((value, *earlier))[0]


def ring_sum(own, send):
    across, up, down = send(own, 2), send(own, 1), send(own, -1)
    return (own.astype(F32) + across.astype(F32)) + (up.astype(F32) + down.astype(F32))


def shards(tile_values, tile_rows, tile_cols, tile_counts, features, weight, cotangent):
    row, col = lax.axis_index("row"), lax.axis_index("col")
    z, yl = row // 2, row % 2
    x, yh, core = col // 4, col // 2 % 2, col % 2
    tiles = tile_values[0, 0]
    t_row, t_col = tile_rows[0, 0], tile_cols[0, 0]
    count = tile_counts[0]

    own, j = t_row // 4, t_row % 4
    dx, dyh, dk = (own // 4 - x) % 4, (own // 2 % 2) ^ yh, (own % 2) ^ core
    row_slot = dk * 32 + dx * 8 + dyh * 4 + j
    own, j = t_col // 4, t_col % 4
    dz, dyl = (own // 2 - z) % 4, (own % 2) ^ yl
    col_slot = dz * 8 + dyl * 4 + j

    own = features.reshape(4, BLK, WIDTH)
    far = yl_swap(own)
    across = z_send(own, 2)
    up, down = z_send(own, -1), z_send(own, 1)
    far_up, far_down = z_send(far, -1), z_send(far, 1)
    far_across = yl_swap(across)
    own = pltpu.with_memory_space_constraint(own, pltpu.HBM)
    pieces = [own, far, up, far_up, across, far_across, down, far_down]

    parts = cell_product("forward_cell", False, row_slot, col_slot, count, tiles, pieces, 16)
    mine = parts[:8]
    other = [None] * 8
    for i in (5, 3, 7):
        other[i] = core_swap(parts[8 + i])
    for i in (2, 6, 4, 1, 0):
        other[i] = core_swap(after(parts[8 + i], other[7]))
    two = yh_swap(add(mine[5], other[5]))
    up, down = x_send(add(mine[3], other[3]), 1), x_send(add(mine[7], other[7]), -1)
    own_up, own_down = x_send(add(mine[2], other[2]), 1), x_send(add(mine[6], other[6]), -1)
    across = x_send(after(add(mine[4], other[4], two), own_up, own_down), 2)
    far = yh_swap(add(mine[1], other[1], up, down))
    terms = [mine[0], other[0], own_up, own_down, across, far]
    scale = 1.0 / math.sqrt(features.shape[0] * lax.axis_size("row") * lax.axis_size("col"))
    output, own, own_rider = dense(scale, terms, weight, cotangent)

    far_rider = yh_swap(own_rider)
    far = far_rider[:4]
    across = x_send(own, 2)
    up, down = x_send(own, -1), x_send(own, 1)
    far_up, far_down = x_send(far, -1), x_send(far, 1)
    far_across = yh_swap(across)
    pieces = [own, far, up, far_up, across, far_across, down, far_down]
    term = add(own_rider[4:], after(far_rider[4:], up, down))
    near_term = z_pair(term, 1)
    term, near_term, *ready = lax.optimization_barrier((term, near_term, *pieces))
    term = add(term, near_term)
    pieces = [*ready, *(core_swap(v) for v in ready)]
    term = add(term, core_swap(term))
    near_term = z_pair(term, 2)
    back = cell_product("backward_cell", True, col_slot, row_slot, count, tiles, pieces, 8)
    two = yl_swap(back[5])
    up, down = z_send(back[3], 1), z_send(back[7], -1)
    own_up, own_down = z_send(back[2], 1), z_send(back[6], -1)
    across = z_send(after(add(back[4], two), own_up, own_down), 2)
    far = yl_swap(add(back[1], up, down))
    grad_features = add(back[0], own_up, own_down, across, far)
    term = add(term, after(near_term, back[0]))
    term = add(term, yl_swap(term))
    weight_grad = ring_sum(term, x_send).reshape(WIDTH, WIDTH)
    return (output, grad_features.reshape(4 * BLK, WIDTH), weight_grad)


def solution(mesh):
    in_specs = (
        P("row", "col", None, None, None),
        P("row", "col", None),
        P("row", "col", None),
        P("row", "col"),
        P(("col", "row"), None),
        P(),
        P(("row", "col"), None),
    )
    out_specs = (P(("row", "col"), None), P(("col", "row"), None), P())
    return jax.shard_map(shards, mesh=mesh, in_specs=in_specs, out_specs=out_specs, check_vma=False)
```

```python
import functools
import math

import jax
import jax.numpy as jnp
from jax import lax
from jax.experimental import pallas as pl
from jax.experimental.pallas import tpu as pltpu
from jax.sharding import PartitionSpec as P

BLK = 128
WIDTH = 256
CAP = 128
UNROLL = 32
CHUNKS = 4
BF16 = jnp.bfloat16
F32 = jnp.float32

NZ, NX = 4, 4


def z_perm(step):
    return [(z * 2 + yl, (z + step) % NZ * 2 + yl) for z in range(NZ) for yl in range(2)]


def yl_perm():
    return [(r, r ^ 1) for r in range(2 * NZ)]


def x_perm(step):
    return [(x * 4 + q, (x + step) % NX * 4 + q) for x in range(NX) for q in range(4)]


def yh_perm():
    return [(c, c ^ 2) for c in range(4 * NX)]


def core_perm():
    return [(c, c ^ 1) for c in range(4 * NX)]


def z_send(v, step):
    return lax.ppermute(v, "row", z_perm(step))


def z_pair(v, flip):
    return lax.ppermute(v, "row", [(r, r ^ (2 * flip)) for r in range(2 * NZ)])


def yl_swap(v):
    return lax.ppermute(v, "row", yl_perm())


def x_send(v, step):
    return lax.ppermute(v, "col", x_perm(step))


def yh_swap(v):
    return lax.ppermute(v, "col", yh_perm())


def core_swap(v):
    return lax.ppermute(v, "col", core_perm())


def add(*terms):
    total = terms[0].astype(F32)
    for term in terms[1:]:
        total = total + term.astype(F32)
    return total.astype(BF16)


def tile_copies(tiles_hbm, tiles, sems):
    size = CAP // CHUNKS
    return [
        pltpu.make_async_copy(
            tiles_hbm.at[pl.ds(c * size, size)], tiles.at[pl.ds(c * size, size)], sems.at[c]
        )
        for c in range(CHUNKS)
    ]


def cell_kernel(transposed, n_in, n_out, out_ref, in_ref, cnt_ref, tiles_hbm, *rest):
    pieces = rest[:n_in]
    outs = rest[n_in : n_in + n_out]
    tiles, blocks, acc, tile_sems, piece_sems = rest[n_in + n_out :]
    copies = [
        pltpu.make_async_copy(piece, blocks.at[pl.ds(4 * i, 4)], piece_sems.at[i])
        for i, piece in enumerate(pieces)
    ]
    loads = tile_copies(tiles_hbm, tiles, tile_sems)
    for copy in copies[:1] + loads[:1] + copies[1:] + loads[1:]:
        copy.start()

    def clear(i, carry):
        acc[i] = jnp.zeros(acc.shape[1:], acc.dtype)
        return carry

    lax.fori_loop(0, acc.shape[0] - 1, clear, 0)
    for copy in copies:
        copy.wait()
    dims = (((0,), (0,)), ((), ())) if transposed else (((1,), (0,)), ((), ()))

    def group(i, carry):
        first = i * UNROLL
        for u in range(UNROLL):
            slot = out_ref[first + u]
            acc[slot] += lax.dot_general(
                tiles[first + u], blocks[in_ref[first + u]], dims, preferred_element_type=F32
            )
        return carry

    groups = (cnt_ref[0] + UNROLL - 1) // UNROLL
    size = CAP // CHUNKS // UNROLL
    for c, load in enumerate(loads):
        load.wait()
        lax.fori_loop(c * size, jnp.clip(groups, c * size, (c + 1) * size), group, 0)
    for o, out in enumerate(outs):
        def store(i, carry, out=out, o=o):
            out[i] = acc[4 * o + i].astype(BF16)
            return carry

        lax.fori_loop(0, 4, store, 0)


def cell_product(name, transposed, out_slot, in_slot, count, tiles, pieces, n_out):
    live = jnp.arange(CAP, dtype=jnp.int32) < count[0]
    out_slot = jnp.where(live, out_slot, 4 * n_out)
    in_slot = jnp.where(live, in_slot, 0)
    any_spec = pl.BlockSpec(memory_space=pl.ANY)
    vmem_spec = pl.BlockSpec(memory_space=pltpu.VMEM)
    return pl.pallas_call(
        functools.partial(cell_kernel, transposed, len(pieces), n_out),
        grid_spec=pltpu.PrefetchScalarGridSpec(
            num_scalar_prefetch=3,
            grid=(),
            in_specs=[any_spec] * (1 + len(pieces)),
            out_specs=[vmem_spec] * n_out,
            scratch_shapes=[
                pltpu.VMEM((CAP, BLK, BLK), BF16),
                pltpu.VMEM((4 * len(pieces), BLK, WIDTH), BF16),
                pltpu.VMEM((4 * n_out + 1, BLK, WIDTH), F32),
                pltpu.SemaphoreType.DMA((CHUNKS,)),
                pltpu.SemaphoreType.DMA((len(pieces),)),
            ],
        ),
        out_shape=[jax.ShapeDtypeStruct((4, BLK, WIDTH), BF16)] * n_out,
        compiler_params=pltpu.CompilerParams(vmem_limit_bytes=(19 if len(pieces) == 8 else 16) * 1024 * 1024),
        cost_estimate=pl.CostEstimate(
            flops=2 * CAP * BLK * BLK * WIDTH,
            bytes_accessed=2 * CAP * BLK * BLK + 8 * (len(pieces) + n_out) * BLK * WIDTH,
            transcendentals=0,
        ),
        name=name,
    )(out_slot, in_slot, count, pltpu.with_memory_space_constraint(tiles, pltpu.HBM), *pieces)


def dense_kernel(scale, n_terms, *refs):
    terms, (w_ref, cot_ref, out_ref, grad_ref, rider_ref) = refs[:n_terms], refs[n_terms:]
    total = terms[0][...].astype(F32)
    for term in terms[1:]:
        total = total + term[...].astype(F32)
    w = w_ref[...]
    agg = total.astype(BF16).reshape(cot_ref.shape)
    pre = jnp.dot(agg, w, preferred_element_type=F32)
    sig = jax.nn.sigmoid(pre)
    out_ref[...] = (pre * sig).astype(BF16)
    grad_pre = (cot_ref[...].astype(F32) * sig * (1.0 + pre * (1.0 - sig))).astype(BF16)
    grad_agg = lax.dot_general(
        grad_pre, w, (((1,), (1,)), ((), ())), preferred_element_type=F32
    ).astype(BF16)
    grad_agg = grad_agg.reshape(grad_ref.shape)
    grad_ref[...] = grad_agg
    rider_ref[pl.ds(0, 4)] = grad_agg
    weight_grad = lax.dot_general(
        agg, grad_pre, (((0,), (0,)), ((), ())), preferred_element_type=F32
    )
    rider_ref[pl.ds(4, 2)] = (weight_grad * scale).astype(BF16).reshape(2, BLK, WIDTH)


def dense(scale, terms, weight, cotangent):
    vmem_spec = pl.BlockSpec(memory_space=pltpu.VMEM)
    nodes = cotangent.shape[0]
    return pl.pallas_call(
        functools.partial(dense_kernel, scale, len(terms)),
        in_specs=[vmem_spec] * (len(terms) + 2),
        out_specs=[vmem_spec] * 3,
        out_shape=[
            jax.ShapeDtypeStruct((nodes, WIDTH), BF16),
            jax.ShapeDtypeStruct((nodes // BLK, BLK, WIDTH), BF16),
            jax.ShapeDtypeStruct((nodes // BLK + 2, BLK, WIDTH), BF16),
        ],
        compiler_params=pltpu.CompilerParams(vmem_limit_bytes=24 * 1024 * 1024),
        cost_estimate=pl.CostEstimate(
            flops=6 * nodes * WIDTH * WIDTH,
            bytes_accessed=8 * nodes * WIDTH,
            transcendentals=nodes * WIDTH,
        ),
        name="dense",
    )(*terms, weight, cotangent)


def after(value, *earlier):
    return lax.optimization_barrier((value, *earlier))[0]


def ring_sum(own, send):
    across, up, down = send(own, 2), send(own, 1), send(own, -1)
    return (own.astype(F32) + across.astype(F32)) + (up.astype(F32) + down.astype(F32))


def shards(tile_values, tile_rows, tile_cols, tile_counts, features, weight, cotangent):
    row, col = lax.axis_index("row"), lax.axis_index("col")
    z, yl = row // 2, row % 2
    x, yh, core = col // 4, col // 2 % 2, col % 2
    tiles = tile_values[0, 0]
    t_row, t_col = tile_rows[0, 0], tile_cols[0, 0]
    count = tile_counts[0]

    own, j = t_row // 4, t_row % 4
    dx, dyh, dk = (own // 4 - x) % 4, (own // 2 % 2) ^ yh, (own % 2) ^ core
    row_slot = dk * 32 + dx * 8 + dyh * 4 + j
    own, j = t_col // 4, t_col % 4
    dz, dyl = (own // 2 - z) % 4, (own % 2) ^ yl
    col_slot = dz * 8 + dyl * 4 + j

    own = features.reshape(4, BLK, WIDTH)
    far = yl_swap(own)
    across = z_send(own, 2)
    up, down = z_send(own, -1), z_send(own, 1)
    far_up, far_down = z_send(far, -1), z_send(far, 1)
    far_across = yl_swap(across)
    own = pltpu.with_memory_space_constraint(own, pltpu.HBM)
    pieces = [own, far, up, far_up, across, far_across, down, far_down]

    parts = cell_product("forward_cell", False, row_slot, col_slot, count, tiles, pieces, 16)
    mine = parts[:8]
    other = [None] * 8
    for i in (5, 3, 7):
        other[i] = core_swap(parts[8 + i])
    for i in (2, 6, 4, 1, 0):
        other[i] = core_swap(after(parts[8 + i], other[7]))
    two = yh_swap(add(mine[5], other[5]))
    up, down = x_send(add(mine[3], other[3]), 1), x_send(add(mine[7], other[7]), -1)
    own_up, own_down = x_send(add(mine[2], other[2]), 1), x_send(add(mine[6], other[6]), -1)
    across = x_send(add(mine[4], other[4], two), 2)
    far = yh_swap(add(mine[1], other[1], up, down))
    terms = [mine[0], other[0], own_up, own_down, across, far]
    scale = 1.0 / math.sqrt(features.shape[0] * lax.axis_size("row") * lax.axis_size("col"))
    output, own, own_rider = dense(scale, terms, weight, cotangent)

    far_rider = yh_swap(own_rider)
    far = far_rider[:4]
    across = x_send(own, 2)
    up, down = x_send(own, -1), x_send(own, 1)
    far_up, far_down = x_send(far, -1), x_send(far, 1)
    far_across = yh_swap(across)
    pieces = [own, far, up, far_up, across, far_across, down, far_down]
    term = add(own_rider[4:], after(far_rider[4:], up, down))
    near_term = z_pair(term, 1)
    term, near_term, *ready = lax.optimization_barrier((term, near_term, *pieces))
    ready = pieces
    term = add(term, near_term)
    pieces = [*ready, *(core_swap(v) for v in ready)]
    term = add(term, core_swap(term))
    near_term = z_pair(term, 2)
    back = cell_product("backward_cell", True, col_slot, row_slot, count, tiles, pieces, 8)
    two = yl_swap(back[5])
    up, down = z_send(back[3], 1), z_send(back[7], -1)
    own_up, own_down = z_send(back[2], 1), z_send(back[6], -1)
    across = z_send(after(add(back[4], two), own_up, own_down), 2)
    far = yl_swap(add(back[1], up, down))
    grad_features = add(back[0], own_up, own_down, across, far)
    term = add(term, after(near_term, back[0]))
    term = add(term, yl_swap(term))
    weight_grad = ring_sum(term, x_send).reshape(WIDTH, WIDTH)
    return (output, grad_features.reshape(4 * BLK, WIDTH), weight_grad)


def solution(mesh):
    in_specs = (
        P("row", "col", None, None, None),
        P("row", "col", None),
        P("row", "col", None),
        P("row", "col"),
        P(("col", "row"), None),
        P(),
        P(("row", "col"), None),
    )
    out_specs = (P(("row", "col"), None), P(("col", "row"), None), P())
    return jax.shard_map(shards, mesh=mesh, in_specs=in_specs, out_specs=out_specs, check_vma=False)
```

```python
import functools
import math

import jax
import jax.numpy as jnp
from jax import lax
from jax.experimental import pallas as pl
from jax.experimental.pallas import tpu as pltpu
from jax.sharding import PartitionSpec as P

BLK = 128
WIDTH = 256
CAP = 128
UNROLL = 32
CHUNKS = 4
BF16 = jnp.bfloat16
F32 = jnp.float32

NZ, NX = 4, 4


def z_perm(step):
    return [(z * 2 + yl, (z + step) % NZ * 2 + yl) for z in range(NZ) for yl in range(2)]


def yl_perm():
    return [(r, r ^ 1) for r in range(2 * NZ)]


def x_perm(step):
    return [(x * 4 + q, (x + step) % NX * 4 + q) for x in range(NX) for q in range(4)]


def yh_perm():
    return [(c, c ^ 2) for c in range(4 * NX)]


def core_perm():
    return [(c, c ^ 1) for c in range(4 * NX)]


def z_send(v, step):
    return lax.ppermute(v, "row", z_perm(step))


def z_pair(v, flip):
    return lax.ppermute(v, "row", [(r, r ^ (2 * flip)) for r in range(2 * NZ)])


def yl_swap(v):
    return lax.ppermute(v, "row", yl_perm())


def x_send(v, step):
    return lax.ppermute(v, "col", x_perm(step))


def yh_swap(v):
    return lax.ppermute(v, "col", yh_perm())


def core_swap(v):
    return lax.ppermute(v, "col", core_perm())


def add(*terms):
    total = terms[0].astype(F32)
    for term in terms[1:]:
        total = total + term.astype(F32)
    return total.astype(BF16)


def tile_copies(tiles_hbm, tiles, sems):
    size = CAP // CHUNKS
    return [
        pltpu.make_async_copy(
            tiles_hbm.at[pl.ds(c * size, size)], tiles.at[pl.ds(c * size, size)], sems.at[c]
        )
        for c in range(CHUNKS)
    ]


def cell_kernel(transposed, n_in, n_out, out_ref, in_ref, cnt_ref, tiles_hbm, *rest):
    pieces = rest[:n_in]
    outs = rest[n_in : n_in + n_out]
    tiles, blocks, acc, tile_sems, piece_sems = rest[n_in + n_out :]
    copies = [
        pltpu.make_async_copy(piece, blocks.at[pl.ds(4 * i, 4)], piece_sems.at[i])
        for i, piece in enumerate(pieces)
    ]
    loads = tile_copies(tiles_hbm, tiles, tile_sems)
    for copy in copies[:1] + loads[:1] + copies[1:] + loads[1:]:
        copy.start()

    def clear(i, carry):
        acc[i] = jnp.zeros(acc.shape[1:], acc.dtype)
        return carry

    lax.fori_loop(0, acc.shape[0] - 1, clear, 0)
    for copy in copies:
        copy.wait()
    dims = (((0,), (0,)), ((), ())) if transposed else (((1,), (0,)), ((), ()))

    def group(i, carry):
        first = i * UNROLL
        for u in range(UNROLL):
            slot = out_ref[first + u]
            acc[slot] += lax.dot_general(
                tiles[first + u], blocks[in_ref[first + u]], dims, preferred_element_type=F32
            )
        return carry

    groups = (cnt_ref[0] + UNROLL - 1) // UNROLL
    size = CAP // CHUNKS // UNROLL
    for c, load in enumerate(loads):
        load.wait()
        lax.fori_loop(c * size, jnp.clip(groups, c * size, (c + 1) * size), group, 0)
    first = 0
    for out in outs:
        def store(i, carry, out=out, first=first):
            out[i] = acc[first + i].astype(BF16)
            return carry

        lax.fori_loop(0, out.shape[0], store, 0)
        first += out.shape[0]


def cell_product(name, transposed, out_slot, in_slot, count, tiles, pieces, sizes):
    n_out, out_blocks = len(sizes), sum(sizes)
    live = jnp.arange(CAP, dtype=jnp.int32) < count[0]
    out_slot = jnp.where(live, out_slot, out_blocks)
    in_slot = jnp.where(live, in_slot, 0)
    any_spec = pl.BlockSpec(memory_space=pl.ANY)
    vmem_spec = pl.BlockSpec(memory_space=pltpu.VMEM)
    return pl.pallas_call(
        functools.partial(cell_kernel, transposed, len(pieces), n_out),
        grid_spec=pltpu.PrefetchScalarGridSpec(
            num_scalar_prefetch=3,
            grid=(),
            in_specs=[any_spec] * (1 + len(pieces)),
            out_specs=[vmem_spec] * n_out,
            scratch_shapes=[
                pltpu.VMEM((CAP, BLK, BLK), BF16),
                pltpu.VMEM((4 * len(pieces), BLK, WIDTH), BF16),
                pltpu.VMEM((out_blocks + 1, BLK, WIDTH), F32),
                pltpu.SemaphoreType.DMA((CHUNKS,)),
                pltpu.SemaphoreType.DMA((len(pieces),)),
            ],
        ),
        out_shape=[jax.ShapeDtypeStruct((size, BLK, WIDTH), BF16) for size in sizes],
        compiler_params=pltpu.CompilerParams(vmem_limit_bytes=(19 if len(pieces) == 8 else 16) * 1024 * 1024),
        cost_estimate=pl.CostEstimate(
            flops=2 * CAP * BLK * BLK * WIDTH,
            bytes_accessed=2 * CAP * BLK * BLK + 2 * (4 * len(pieces) + out_blocks) * BLK * WIDTH,
            transcendentals=0,
        ),
        name=name,
    )(out_slot, in_slot, count, pltpu.with_memory_space_constraint(tiles, pltpu.HBM), *pieces)


def dense_kernel(scale, n_terms, *refs):
    terms, (w_ref, cot_ref, out_ref, grad_ref, rider_ref) = refs[:n_terms], refs[n_terms:]
    total = terms[0][...].astype(F32)
    for term in terms[1:]:
        total = total + term[...].astype(F32)
    w = w_ref[...]
    agg = total.astype(BF16).reshape(cot_ref.shape)
    pre = jnp.dot(agg, w, preferred_element_type=F32)
    sig = jax.nn.sigmoid(pre)
    out_ref[...] = (pre * sig).astype(BF16)
    grad_pre = (cot_ref[...].astype(F32) * sig * (1.0 + pre * (1.0 - sig))).astype(BF16)
    grad_agg = lax.dot_general(
        grad_pre, w, (((1,), (1,)), ((), ())), preferred_element_type=F32
    ).astype(BF16)
    grad_agg = grad_agg.reshape(grad_ref.shape)
    grad_ref[...] = grad_agg
    rider_ref[pl.ds(0, 4)] = grad_agg
    weight_grad = lax.dot_general(
        agg, grad_pre, (((0,), (0,)), ((), ())), preferred_element_type=F32
    )
    rider_ref[pl.ds(4, 2)] = (weight_grad * scale).astype(BF16).reshape(2, BLK, WIDTH)


def dense(scale, terms, weight, cotangent):
    vmem_spec = pl.BlockSpec(memory_space=pltpu.VMEM)
    nodes = cotangent.shape[0]
    return pl.pallas_call(
        functools.partial(dense_kernel, scale, len(terms)),
        in_specs=[vmem_spec] * (len(terms) + 2),
        out_specs=[vmem_spec] * 3,
        out_shape=[
            jax.ShapeDtypeStruct((nodes, WIDTH), BF16),
            jax.ShapeDtypeStruct((nodes // BLK, BLK, WIDTH), BF16),
            jax.ShapeDtypeStruct((nodes // BLK + 2, BLK, WIDTH), BF16),
        ],
        compiler_params=pltpu.CompilerParams(vmem_limit_bytes=24 * 1024 * 1024),
        cost_estimate=pl.CostEstimate(
            flops=6 * nodes * WIDTH * WIDTH,
            bytes_accessed=8 * nodes * WIDTH,
            transcendentals=nodes * WIDTH,
        ),
        name="dense",
    )(*terms, weight, cotangent)


def after(value, *earlier):
    return lax.optimization_barrier((value, *earlier))[0]


def ring_sum(own, send):
    across, up, down = send(own, 2), send(own, 1), send(own, -1)
    return (own.astype(F32) + across.astype(F32)) + (up.astype(F32) + down.astype(F32))


def shards(tile_values, tile_rows, tile_cols, tile_counts, features, weight, cotangent):
    row, col = lax.axis_index("row"), lax.axis_index("col")
    z, yl = row // 2, row % 2
    x, yh, core = col // 4, col // 2 % 2, col % 2
    tiles = tile_values[0, 0]
    t_row, t_col = tile_rows[0, 0], tile_cols[0, 0]
    count = tile_counts[0]

    own, j = t_row // 4, t_row % 4
    dx, dyh, dk = (own // 4 - x) % 4, (own // 2 % 2) ^ yh, (own % 2) ^ core
    row_slot = dk * 32 + dx * 8 + dyh * 4 + j
    piece = dx * 2 + dyh
    rank = sum(jnp.where(piece == i, n, 0) for i, n in enumerate((7, 6, 3, 1, 5, 0, 4, 2)))
    row_out = jnp.where(dk == 0, row_slot, 32 + rank * 4 + j)
    own, j = t_col // 4, t_col % 4
    dz, dyl = (own // 2 - z) % 4, (own % 2) ^ yl
    col_slot = dz * 8 + dyl * 4 + j

    own = features.reshape(4, BLK, WIDTH)
    far = yl_swap(own)
    across = z_send(own, 2)
    up, down = z_send(own, -1), z_send(own, 1)
    far_up, far_down = z_send(far, -1), z_send(far, 1)
    far_across = yl_swap(across)
    own = pltpu.with_memory_space_constraint(own, pltpu.HBM)
    pieces = [own, far, up, far_up, across, far_across, down, far_down]

    parts = cell_product(
        "forward_cell",
        False,
        row_out,
        col_slot,
        count,
        tiles,
        pieces,
        [4] * 8 + [4, 8, 8, 4, 4, 4],
    )
    mine = parts[:8]
    first, near = core_swap(parts[8]), core_swap(parts[9])
    own_near, *rest = [core_swap(after(v, near)) for v in parts[10:]]
    other = [rest[2], rest[1], own_near[:4], near[:4], rest[0], first, own_near[4:], near[4:]]
    two = yh_swap(add(mine[5], other[5]))
    up, down = x_send(add(mine[3], other[3]), 1), x_send(add(mine[7], other[7]), -1)
    own_up, own_down = x_send(add(mine[2], other[2]), 1), x_send(add(mine[6], other[6]), -1)
    across = x_send(add(mine[4], other[4], two), 2)
    far = yh_swap(add(mine[1], other[1], up, down))
    terms = [mine[0], other[0], own_up, own_down, across, far]
    scale = 1.0 / math.sqrt(features.shape[0] * lax.axis_size("row") * lax.axis_size("col"))
    output, own, own_rider = dense(scale, terms, weight, cotangent)

    far_rider = yh_swap(own_rider)
    far = far_rider[:4]
    across = x_send(own, 2)
    up, down = x_send(own, -1), x_send(own, 1)
    far_up, far_down = x_send(far, -1), x_send(far, 1)
    far_across = yh_swap(across)
    pieces = [own, far, up, far_up, across, far_across, down, far_down]
    term = add(own_rider[4:], after(far_rider[4:], up, down))
    near_term = z_pair(term, 1)
    term, near_term, *ready = lax.optimization_barrier((term, near_term, *pieces))
    ready = pieces
    term = add(term, near_term)
    pieces = [*ready, *(core_swap(v) for v in ready)]
    term = add(term, core_swap(term))
    near_term = z_pair(term, 2)
    back = cell_product("backward_cell", True, col_slot, row_slot, count, tiles, pieces, [4] * 8)
    two = yl_swap(back[5])
    up, down = z_send(back[3], 1), z_send(back[7], -1)
    own_up, own_down = z_send(back[2], 1), z_send(back[6], -1)
    across = z_send(after(add(back[4], two), own_up, own_down), 2)
    far = yl_swap(add(back[1], up, down))
    grad_features = add(back[0], own_up, own_down, across, far)
    term = add(term, after(near_term, back[0]))
    term = add(term, yl_swap(term))
    weight_grad = ring_sum(term, x_send).reshape(WIDTH, WIDTH)
    return (output, grad_features.reshape(4 * BLK, WIDTH), weight_grad)


def solution(mesh):
    in_specs = (
        P("row", "col", None, None, None),
        P("row", "col", None),
        P("row", "col", None),
        P("row", "col"),
        P(("col", "row"), None),
        P(),
        P(("row", "col"), None),
    )
    out_specs = (P(("row", "col"), None), P(("col", "row"), None), P())
    return jax.shard_map(shards, mesh=mesh, in_specs=in_specs, out_specs=out_specs, check_vma=False)
```
